32 devices in a mesh: front: 4 (over z), row: 4 (over x, core), col: 2 (over y).
Axes of the slice: x: 2, y: 2, z: 4, core: 2. Of those that a mesh axis runs over, the one named last changes fastest.
Arguments:
- front_orig: float32 [4, 8192, 8192], P('front', 'row', 'col'), may hold values from -6 to 6
- children: float32 [4, 2048, 2048], P('front', 'row', 'col'), may hold values from -6 to 6
- parent_of: int32 [4], P('front'), may hold values from 0 to 3, as said below
- child_map: int32 [4, 8], P('front'), may hold values from 0 to 31, as said below
- block_mask: int32 [4, 32, 32], P('front'), may hold values 0 or 1
- pivot: int32 [4, 32], P('front'), may hold values from 0 to 31, each once within a row
- diag_inverse: float32 [4, 2, 512, 512], P('front'), may hold values from -0.01171875 to 0.01171875
Outputs:
- factored: float32 [4, 8192, 8192], P('front', 'row', 'col')
The draws below stay inside these ranges and needn't reach their ends.
Inputs may be any that keep to these rules, and one draw needn't show every extreme that they name: `parent_of`: each front is the parent of exactly one child update. Each row of child_map is strictly increasing.
All inputs are finite; a program needn't handle non-finite values. No bound on the sum of `block_mask` on one device may be relied on, other than what follows from the above.
Results may differ from the reference program's by a relative error of at most 0.00011.
Values sent between devices are 32-bit elements; how exact they have to be, the bound alone decides.
A program may use at most 256 MiB of HBM per device.

```python
import jax
import jax.numpy as jnp
from jax import lax

BS = 256
F = 8192
PANELS = 2
KIDS = 1
NB = 32
CB = 8
CU = 2048
PW = 512
NFR = 4
NCH = 4
N_ROW = 4


def draw_parent_of(key, part):
    owners = jnp.repeat(jnp.arange(NFR, dtype=jnp.int32), KIDS)
    owners = jax.random.permutation(key, owners).astype(jnp.int32)
    target = NFR // 2 * KIDS
    found = jnp.argmax((owners == 0).astype(jnp.int32)).astype(jnp.int32)
    moved = owners[target]
    owners = owners.at[found].set(moved).at[target].set(0)
    return owners.astype(jnp.int32)


def draw_child_map(key, part):

    def one_child(index):
        picks = jax.random.permutation(jax.random.fold_in(key, index), NB)[:CB]
        return jnp.sort(picks.astype(jnp.int32))
    rows_all = jax.vmap(one_child)(jnp.arange(NCH, dtype=jnp.int32))
    low_span = NB // N_ROW
    low_picks = jax.random.permutation(jax.random.fold_in(key, 7919), low_span - 1)[:CB // 2].astype(jnp.int32) + 1
    high_picks = jax.random.permutation(jax.random.fold_in(key, 7927), NB - low_span - 1)[:CB // 2 - 2].astype(jnp.int32) + low_span
    ends = jnp.array([0, NB - 1], jnp.int32)
    first_row = jnp.sort(jnp.concatenate([ends, low_picks, high_picks]))
    return rows_all.at[0].set(first_row).astype(jnp.int32)


def plant(drawn, stream_key, least, top_value):
    extent = drawn.shape
    spot = [jax.random.randint(jax.random.fold_in(stream_key, axis), (), 0, extent[axis]) for axis in range(len(extent))]
    drawn = drawn.at[tuple(spot)].set(least)
    longest = extent.index(max(extent))
    spot[longest] = (spot[longest] + 1) % extent[longest]
    return drawn.at[tuple(spot)].set(top_value)


def level_of(stream_key, shape, split, low, top_value):
    loudness = 1.0
    for dim, blocks in split:
        steps = jax.random.uniform(jax.random.fold_in(jax.random.fold_in(stream_key, 6), dim), (blocks,), jnp.float32, low / len(split), top_value / len(split))
        loudness = loudness * jnp.repeat(jnp.exp(steps), shape[dim] // blocks).reshape((-1,) + (1,) * (len(shape) - 1 - dim))
    return loudness


def gaussian(own_key, dims, width, limit, cuts=(), held_as=jnp.bfloat16):
    values = width * jax.random.normal(own_key, dims, jnp.float32)
    if cuts:
        values = values * level_of(own_key, dims, cuts, -0.22, 0.18)
    return jnp.clip(values, -limit, limit).astype(held_as)


def setup_inputs(seed: int = 0) -> dict:
    keys = jax.random.split(jax.random.key(seed), 8)
    return {
        "front_orig": gaussian(keys[0], (NFR, F, F), 1.0, 6.0, ((0, 4), (1, 4), (2, 2)), jnp.float32),
        "children": gaussian(keys[1], (NCH, CU, CU), 1.0, 6.0, ((0, 4), (1, 4), (2, 2)), jnp.float32),
        "parent_of": draw_parent_of(jax.random.fold_in(keys[7], 71), 0),
        "child_map": draw_child_map(jax.random.fold_in(keys[7], 71), 0),
        "block_mask": plant((jax.random.randint(keys[4], (NFR, NB, NB), 0, 4) < 3).astype(jnp.int32), jax.random.fold_in(keys[4], 1), 0, 1),
        "pivot": jax.vmap(lambda own: jax.random.permutation(own, NB))(jax.random.split(keys[5], NFR)).reshape((NFR, NB)).astype(jnp.int32),
        "diag_inverse": gaussian(keys[6], (NFR, PANELS, PW, PW), (PW * PW) ** -0.5, 0.01171875, ((0, 4),), jnp.float32),
    }


HIGH = lax.Precision.HIGHEST


def place(update, mapping):
    nblocks = F // BS
    tiles = update.reshape(CB, BS, CB, BS).transpose(0, 2, 1, 3)
    grid = jnp.zeros((nblocks, nblocks, BS, BS), jnp.float32).at[mapping[:, None], mapping[None, :]].set(tiles)
    return grid.transpose(0, 2, 1, 3).reshape(F, F)


def spread(grid):
    return jnp.repeat(jnp.repeat(grid, BS, axis=0), BS, axis=1)


def reference(front_orig, children, parent_of, child_map, block_mask, pivot, diag_inverse):
    nblocks = F // BS

    def add_child(total, item):
        update, owner, mapping = item
        placed = place(update, mapping)
        return total.at[owner].add(placed), None

    extended, _ = lax.scan(add_child, jnp.zeros((NFR, F, F), jnp.float32), (children, parent_of, child_map))
    results = []
    ranks = jnp.arange(nblocks, dtype=jnp.int32)
    for front in range(NFR):
        mask = block_mask[front].astype(jnp.float32)
        matrix = spread(mask) * (front_orig[front] + extended[front])
        order = pivot[front]
        position = jnp.sum(jnp.where(order[:, None] == ranks[None, :], ranks[:, None], 0), axis=0).astype(jnp.int32)
        for step in range(PANELS):
            alive = (position >= 2 * step + 2).astype(jnp.float32)
            live = jnp.repeat(alive, BS)
            first = order[2 * step]
            second = order[2 * step + 1]
            column_panel = jnp.concatenate([lax.dynamic_slice_in_dim(matrix, first * BS, BS, 1), lax.dynamic_slice_in_dim(matrix, second * BS, BS, 1)], axis=1)
            row_panel = jnp.concatenate([lax.dynamic_slice_in_dim(matrix, first * BS, BS, 0), lax.dynamic_slice_in_dim(matrix, second * BS, BS, 0)], axis=0)
            lower = jnp.dot(column_panel, diag_inverse[front, step], precision=HIGH, preferred_element_type=jnp.float32)
            update = jnp.dot(lower * live[:, None], row_panel, precision=HIGH, preferred_element_type=jnp.float32)
            matrix = matrix - update * spread(mask * alive[:, None] * alive[None, :])
            for half, chosen in enumerate((first, second)):
                current = lax.dynamic_slice_in_dim(matrix, chosen * BS, BS, 1)
                written = jnp.where(live[:, None] > 0, lower[:, half * BS:(half + 1) * BS], current)
                matrix = lax.dynamic_update_slice_in_dim(matrix, written, chosen * BS, 1)
        results.append(matrix)
    return jnp.stack(results)
```

```python
import functools

import jax
import jax.numpy as jnp
from jax import lax
from jax.experimental import pallas as pl
from jax.experimental.pallas import tpu as pltpu
from jax.sharding import PartitionSpec as P

BS = 256
PIV = 4
HIGH = lax.Precision.HIGHEST


def split(x):
    hi = x.astype(jnp.bfloat16)
    return hi, (x - hi.astype(jnp.float32)).astype(jnp.bfloat16)


def dot(a, b):
    return jnp.dot(a, b, preferred_element_type=jnp.float32)


def dot3(a, b):
    ah, al = split(a)
    bh, bl = split(b)
    return dot(ah, bh) + (dot(al, bh) + dot(ah, bl))


def lower_kernel(meta, *refs, others, cols):
    cands = refs[: 1 + others]
    kids = refs[1 + others : 1 + others + PIV]
    diag, u01, hi_ref, lo_ref = refs[1 + others + PIV :]
    i = pl.program_id(0)
    parts = []
    for k in range(PIV):
        span = slice(k * BS, (k + 1) * BS)
        value = cands[0][:, span]
        for n in range(others):
            value = jnp.where(meta[0, k] == n + 1, cands[n + 1][:, span], value)
        kid = jnp.where(meta[2, k] * meta[4, i] == 1, kids[k][0, 0], 0.0)
        parts.append(jnp.where(meta[8 + k, i] == 1, value + kid, 0.0))
    low0 = dot3(jnp.concatenate(parts[:2], axis=1), diag[0, 0])
    change = dot3(low0, u01[...])
    nexts = [
        parts[2 + h] - jnp.where(meta[10 + h, i] == 1, change[:, h * BS : (h + 1) * BS], 0.0)
        for h in range(2)
    ]
    low1 = dot3(jnp.concatenate(nexts, axis=1), diag[0, 1])
    hi, lo = split(jnp.concatenate([low0, low1], axis=1))
    hi_ref[...] = hi
    lo_ref[...] = lo


def upper_kernel(meta, own, other, k0, k1, k2, k3, l10, hi_ref, lo_ref):
    j = pl.program_id(0)
    kids = (k0, k1, k2, k3)
    parts = []
    for k in range(PIV):
        value = jnp.where(meta[0, j] == 1, own[k], other[k])
        kid = jnp.where(meta[4, k] * meta[2, j] == 1, kids[k][0, 0], 0.0)
        parts.append(jnp.where(meta[8 + k, j] == 1, value + kid, 0.0))
    up0 = jnp.concatenate(parts[:2], axis=0)
    change = dot3(l10[...], up0)
    nexts = [
        parts[2 + h] - jnp.where(meta[10 + h, j] == 1, change[h * BS : (h + 1) * BS], 0.0)
        for h in range(2)
    ]
    hi, lo = split(jnp.concatenate([up0] + nexts, axis=0))
    hi_ref[...] = hi
    lo_ref[...] = lo


def trail_kernel(rows, cols, kinds, m_ref, slab, lh, ll, rh, rl, out, *, tile, kc):
    i = pl.program_id(0)
    t = pl.program_id(1)
    half = 2 * BS

    @pl.loop(0, tile)
    def _(n):
        j = t * tile + n
        kind = kinds[i, j]
        here = pl.ds(pl.multiple_of(n * BS, BS), BS)
        there = pl.ds(pl.multiple_of(j * BS, BS), BS)

        @pl.when(kind == 0)
        def _():
            out[:, here] = jnp.zeros((BS, BS), jnp.float32)

        def product(depth):
            ah, al = lh[:, :depth], ll[:, :depth]
            bh, bl = rh[:depth, there], rl[:depth, there]
            return dot(ah, bh) + dot(al, bh) + dot(ah, bl)

        @pl.when(kind == 1)
        def _():
            out[:, here] = m_ref[:, here]

        @pl.when(kind == 2)
        def _():
            out[:, here] = m_ref[:, here] - product(half)

        @pl.when(kind == 3)
        def _():
            out[:, here] = m_ref[:, here] - product(2 * half)

        @pl.when((kind >= 1) & (kind < 4) & (rows[0, i] * cols[0, j] == 1))
        def _():
            b = cols[1, j]
            span = pl.ds(pl.multiple_of(b % kc * BS, BS), BS)
            out[:, here] += slab[0, b // kc, :, span]

        @pl.when(kind >= 4)
        def _():
            span = pl.ds(pl.multiple_of((kind - 4) * BS, BS), BS)
            out[:, here] = lh[:, span].astype(jnp.float32) + ll[:, span].astype(jnp.float32)


def body(front_orig, children, parent_of, child_map, block_mask, pivot, diag_inverse):
    f32, i32 = jnp.float32, jnp.int32
    nrow, ncol = lax.axis_size("row"), lax.axis_size("col")
    r, c = lax.axis_index("row"), lax.axis_index("col")
    matrix = front_orig[0]
    loc_rows, loc_cols = matrix.shape
    rb, cb = loc_rows // BS, loc_cols // BS
    kr, kc = children.shape[1] // BS, children.shape[2] // BS
    nb = block_mask.shape[1]
    order = pivot[0]
    mask = block_mask[0]

    col_slot = [order[k] % cb for k in range(PIV)]
    row_slot = [order[k] % rb for k in range(PIV)]
    mine_c = jnp.concatenate(
        [lax.dynamic_slice(matrix, (0, col_slot[k] * BS), (loc_rows, BS)) for k in range(PIV)], axis=1
    )
    cands = [mine_c] + [
        lax.ppermute(mine_c, "col", [(s, (s + n) % ncol) for s in range(ncol)]) for n in range(1, ncol)
    ]

    core = r % 2
    wide = loc_cols // 2
    near = [(s, s ^ 1) for s in range(nrow)]
    halves, others = [], []
    for k in range(PIV):
        owner = order[k] // rb
        start = row_slot[k] * BS
        give = lax.dynamic_slice(matrix, (start, (1 - core) * wide), (BS, wide))
        keep = lax.dynamic_slice(matrix, (start, core * wide), (BS, wide))
        got = lax.ppermute(give, "row", near)
        part = jnp.where(owner % 2 == core, keep, got)
        hop = 2
        while hop < nrow:
            got = lax.ppermute(part, "row", [(s, s ^ hop) for s in range(nrow)])
            part = jnp.where((owner // hop) % 2 == (r // hop) % 2, part, got)
            hop *= 2
        halves.append(part)
        others.append(lax.ppermute(part, "row", near))
    half_own, half_other = jnp.stack(halves), jnp.stack(others)

    parents = lax.all_gather(parent_of, "front", axis=0, tiled=True)
    maps = lax.all_gather(child_map, "front", axis=0, tiled=True)
    pieces = lax.all_gather(children, "front", axis=0, tiled=True)
    owned = jnp.argmax((parents == lax.axis_index("front")).astype(i32)).astype(i32)
    own_map = lax.dynamic_index_in_dim(maps, owned, 0, keepdims=False)
    piece = lax.dynamic_index_in_dim(pieces, owned, 0, keepdims=True)
    kid = lax.all_gather(piece, ("row", "col"), axis=0, tiled=True)
    kid = kid.reshape(nrow, ncol, kr * BS, kc * BS)

    ids = jnp.arange(nb, dtype=i32)
    has = jnp.any(own_map[:, None] == ids[None, :], axis=0).astype(i32)
    src = jnp.maximum(jnp.sum((own_map[:, None] <= ids[None, :]).astype(i32), axis=0) - 1, 0)
    position = jnp.sum(jnp.where(order[:, None] == ids[None, :], ids[:, None], 0), axis=0).astype(i32)

    def rows_of(x):
        return lax.dynamic_slice_in_dim(x, r * rb, rb)

    def cols_of(x):
        return lax.dynamic_slice_in_dim(x, c * cb, cb)

    def picked(x):
        hit = (order[:PIV, None] == ids[None, :]).astype(i32)
        return jnp.sum(hit * x[None, :], axis=1)

    hit = (order[:PIV, None] == ids[None, :]).astype(i32)
    mask_cols = jnp.sum(hit[:, :, None] * mask.T[None], axis=1)
    mask_rows = jnp.sum(hit[:, :, None] * mask[None], axis=1)
    pos_r, pos_c = rows_of(position)[:, None], cols_of(position)[None, :]
    local_mask = lax.dynamic_slice(mask, (r * rb, c * cb), (rb, cb))
    kinds = jnp.where((pos_r >= 2) & (pos_c >= 2), 2, 1)
    kinds = jnp.where((pos_r >= 4) & (pos_c >= 4), 3, kinds)
    kinds = jnp.where(local_mask > 0, kinds, 0)
    kinds = jnp.where((pos_c < PIV) & (pos_r >= pos_c // 2 * 2 + 2), 4 + pos_c, kinds).astype(i32)

    def corner(x, y):
        orr, occ = order[x], order[y]
        block = lax.dynamic_slice(matrix, (row_slot[x] * BS, col_slot[y] * BS), (BS, BS))
        return jnp.where((orr // rb == r) & (occ // cb == c), block, 0.0)

    def square(make, xs, ys):
        return jnp.concatenate([jnp.concatenate([make(x, y) for y in ys], axis=1) for x in xs], axis=0)

    corners = lax.psum(
        jnp.stack([square(corner, (0, 1), (2, 3)), square(corner, (2, 3), (0, 1))]), ("row", "col")
    )
    psrc, phas = picked(src), picked(has)

    def kid_corner(x, y):
        a, b = psrc[x], psrc[y]
        block = lax.dynamic_slice(kid, (a // kr, b // kc, a % kr * BS, b % kc * BS), (1, 1, BS, BS))
        return jnp.where(phas[x] * phas[y] == 1, block[0, 0], 0.0)

    def mask_corner(x, y):
        return jnp.broadcast_to(picked(mask_rows[x])[y], (BS, BS)).astype(f32)

    u01 = (corners[0] + square(kid_corner, (0, 1), (2, 3))) * square(mask_corner, (0, 1), (2, 3))
    a10 = (corners[1] + square(kid_corner, (2, 3), (0, 1))) * square(mask_corner, (2, 3), (0, 1))
    l10 = jnp.dot(a10, diag_inverse[0, 0], precision=HIGH, preferred_element_type=f32)

    def pad(rows, n):
        return jnp.pad(rows.astype(i32), (0, n - rows.shape[0]))

    n = max(rb, PIV)
    zero = jnp.zeros((n,), i32)
    shift = jnp.stack([(c - order[k] // cb) % ncol for k in range(PIV)])
    meta = jnp.stack(
        [pad(shift, n), pad(psrc, n), pad(phas, n), pad(rows_of(src), n), pad(rows_of(has), n)]
        + [zero] * 3
        + [pad(rows_of(mask_cols[k]), n) for k in range(PIV)]
    )
    params = pltpu.CompilerParams(vmem_limit_bytes=52 * 2**20)

    def kid_spec(k):
        def where(i, m):
            a, b = m[3, i], m[1, k]
            return a // kr, b // kc, a % kr, b % kc

        return pl.BlockSpec((1, 1, BS, BS), where)

    low_h, low_l = pl.pallas_call(
        functools.partial(lower_kernel, others=ncol - 1, cols=cb),
        grid_spec=pltpu.PrefetchScalarGridSpec(
            num_scalar_prefetch=1,
            grid=(rb,),
            in_specs=[pl.BlockSpec((BS, PIV * BS), lambda i, m: (i, 0))] * ncol
            + [kid_spec(k) for k in range(PIV)]
            + [
                pl.BlockSpec((1, 2, 2 * BS, 2 * BS), lambda i, m: (0, 0, 0, 0)),
                pl.BlockSpec((2 * BS, 2 * BS), lambda i, m: (0, 0)),
            ],
            out_specs=[pl.BlockSpec((BS, PIV * BS), lambda i, m: (i, 0))] * 2,
        ),
        out_shape=[jax.ShapeDtypeStruct((loc_rows, PIV * BS), jnp.bfloat16)] * 2,
        compiler_params=params,
        name="lower",
    )(meta, *cands, *[kid] * PIV, diag_inverse, u01)

    n = max(cb, PIV)
    zero = jnp.zeros((n,), i32)
    held = (jnp.arange(cb, dtype=i32) // (cb // 2) == core).astype(i32)
    meta = jnp.stack(
        [pad(held, n), pad(cols_of(src), n), pad(cols_of(has), n), pad(psrc, n), pad(phas, n)]
        + [zero] * 3
        + [pad(cols_of(mask_rows[k]), n) for k in range(PIV)]
    )

    def kid_spec_up(k):
        def where(j, m):
            a, b = m[3, k], m[1, j]
            return a // kr, b // kc, a % kr, b % kc

        return pl.BlockSpec((1, 1, BS, BS), where)

    up_h, up_l = pl.pallas_call(
        upper_kernel,
        grid_spec=pltpu.PrefetchScalarGridSpec(
            num_scalar_prefetch=1,
            grid=(cb,),
            in_specs=[pl.BlockSpec((PIV, BS, BS), lambda j, m: (0, 0, j % (cb // 2)))] * 2
            + [kid_spec_up(k) for k in range(PIV)]
            + [pl.BlockSpec((2 * BS, 2 * BS), lambda j, m: (0, 0))],
            out_specs=[pl.BlockSpec((PIV * BS, BS), lambda j, m: (0, j))] * 2,
        ),
        out_shape=[jax.ShapeDtypeStruct((PIV * BS, loc_cols), jnp.bfloat16)] * 2,
        compiler_params=params,
        name="upper",
    )(meta, half_own, half_other, *[kid] * PIV, l10)

    tile = min(4, cb)
    rows = jnp.stack([rows_of(has), rows_of(src)])
    cols = jnp.stack([cols_of(has), cols_of(src)])
    out = pl.pallas_call(
        functools.partial(trail_kernel, tile=tile, kc=kc),
        grid_spec=pltpu.PrefetchScalarGridSpec(
            num_scalar_prefetch=3,
            grid=(rb, cb // tile),
            in_specs=[
                pl.BlockSpec((BS, tile * BS), lambda i, t, rows, *_: (i, t)),
                pl.BlockSpec(
                    (1, ncol, BS, kc * BS), lambda i, t, rows, *_: (rows[1, i] // kr, 0, rows[1, i] % kr, 0)
                ),
                pl.BlockSpec((BS, PIV * BS), lambda i, t, *_: (i, 0)),
                pl.BlockSpec((BS, PIV * BS), lambda i, t, *_: (i, 0)),
                pl.BlockSpec(memory_space=pltpu.VMEM),
                pl.BlockSpec(memory_space=pltpu.VMEM),
            ],
            out_specs=pl.BlockSpec((BS, tile * BS), lambda i, t, *_: (i, t)),
        ),
        out_shape=jax.ShapeDtypeStruct((loc_rows, loc_cols), f32),
        compiler_params=params,
        name="trail",
    )(rows, cols, kinds, matrix, kid, low_h, low_l, up_h, up_l)
    return out[None]


def solution(mesh):
    placed = (
        P("front", "row", "col"),
        P("front", "row", "col"),
        P("front"),
        P("front", None),
        P("front", None, None),
        P("front", None),
        P("front", None, None, None),
    )
    return jax.shard_map(
        body, mesh=mesh, in_specs=placed, out_specs=P("front", "row", "col"), check_vma=False
    )
```

```python
import functools

import jax
import jax.numpy as jnp
from jax import lax
from jax.experimental import pallas as pl
from jax.experimental.pallas import tpu as pltpu
from jax.sharding import PartitionSpec as P

BS = 256
PIV = 4
HIGH = lax.Precision.HIGHEST


def split(x):
    hi = x.astype(jnp.bfloat16)
    return hi, (x - hi.astype(jnp.float32)).astype(jnp.bfloat16)


def dot(a, b):
    return jnp.dot(a, b, preferred_element_type=jnp.float32)


def dot3(a, b):
    ah, al = split(a)
    bh, bl = split(b)
    return dot(ah, bh) + (dot(al, bh) + dot(ah, bl))


def lower_kernel(meta, *refs, others, cols):
    cands = refs[: (1 + others) * PIV]
    kids = refs[(1 + others) * PIV : (2 + others) * PIV]
    diag, u01, hi_ref, lo_ref = refs[(2 + others) * PIV :]
    i = pl.program_id(0)
    parts = []
    for k in range(PIV):
        value = cands[k][...]
        for n in range(1, others + 1):
            value = jnp.where(meta[0, k] == n, cands[n * PIV + k][...], value)
        kid = jnp.where(meta[2, k] * meta[4, i] == 1, kids[k][0, 0], 0.0)
        parts.append(jnp.where(meta[8 + k, i] == 1, value + kid, 0.0))
    low0 = dot3(jnp.concatenate(parts[:2], axis=1), diag[0, 0])
    change = dot3(low0, u01[...])
    nexts = [
        parts[2 + h] - jnp.where(meta[10 + h, i] == 1, change[:, h * BS : (h + 1) * BS], 0.0)
        for h in range(2)
    ]
    low1 = dot3(jnp.concatenate(nexts, axis=1), diag[0, 1])
    hi, lo = split(jnp.concatenate([low0, low1], axis=1))
    hi_ref[...] = hi
    lo_ref[...] = lo


def upper_kernel(meta, *refs):
    own, other, kids = refs[:PIV], refs[PIV : 2 * PIV], refs[2 * PIV : 3 * PIV]
    l10, hi_ref, lo_ref = refs[3 * PIV :]
    j = pl.program_id(0)
    parts = []
    for k in range(PIV):
        value = jnp.where(meta[0, j] == 1, own[k][...], other[k][...])
        kid = jnp.where(meta[4, k] * meta[2, j] == 1, kids[k][0, 0], 0.0)
        parts.append(jnp.where(meta[8 + k, j] == 1, value + kid, 0.0))
    up0 = jnp.concatenate(parts[:2], axis=0)
    change = dot3(l10[...], up0)
    nexts = [
        parts[2 + h] - jnp.where(meta[10 + h, j] == 1, change[h * BS : (h + 1) * BS], 0.0)
        for h in range(2)
    ]
    hi, lo = split(jnp.concatenate([up0] + nexts, axis=0))
    hi_ref[...] = hi
    lo_ref[...] = lo


def trail_kernel(rows, cols, kinds, m_ref, slab, lh, ll, rh, rl, out, *, tile, kc):
    i = pl.program_id(0)
    t = pl.program_id(1)
    half = 2 * BS

    @pl.loop(0, tile)
    def _(n):
        j = t * tile + n
        kind = kinds[i, j]
        here = pl.ds(pl.multiple_of(n * BS, BS), BS)
        there = pl.ds(pl.multiple_of(j * BS, BS), BS)

        @pl.when(kind == 0)
        def _():
            out[:, here] = jnp.zeros((BS, BS), jnp.float32)

        def product(depth):
            ah, al = lh[:, :depth], ll[:, :depth]
            bh, bl = rh[:depth, there], rl[:depth, there]
            return dot(ah, bh) + dot(al, bh) + dot(ah, bl)

        @pl.when(kind == 1)
        def _():
            out[:, here] = m_ref[:, here]

        @pl.when(kind == 2)
        def _():
            out[:, here] = m_ref[:, here] - product(half)

        @pl.when(kind == 3)
        def _():
            out[:, here] = m_ref[:, here] - product(2 * half)

        @pl.when((kind >= 1) & (kind < 4) & (rows[0, i] * cols[0, j] == 1))
        def _():
            b = cols[1, j]
            span = pl.ds(pl.multiple_of(b % kc * BS, BS), BS)
            out[:, here] += slab[0, b // kc, :, span]

        @pl.when(kind >= 4)
        def _():
            span = pl.ds(pl.multiple_of((kind - 4) * BS, BS), BS)
            out[:, here] = lh[:, span].astype(jnp.float32) + ll[:, span].astype(jnp.float32)


def body(front_orig, children, parent_of, child_map, block_mask, pivot, diag_inverse):
    f32, i32 = jnp.float32, jnp.int32
    nrow, ncol = lax.axis_size("row"), lax.axis_size("col")
    r, c = lax.axis_index("row"), lax.axis_index("col")
    matrix = front_orig[0]
    loc_rows, loc_cols = matrix.shape
    rb, cb = loc_rows // BS, loc_cols // BS
    kr, kc = children.shape[1] // BS, children.shape[2] // BS
    nb = block_mask.shape[1]
    order = pivot[0]
    mask = block_mask[0]

    col_slot = [order[k] % cb for k in range(PIV)]
    row_slot = [order[k] % rb for k in range(PIV)]
    mine_c = [lax.dynamic_slice(matrix, (0, col_slot[k] * BS), (loc_rows, BS)) for k in range(PIV)]
    cands = [mine_c] + [
        [lax.ppermute(mine_c[k], "col", [(s, (s + n) % ncol) for s in range(ncol)]) for k in range(PIV)]
        for n in range(1, ncol)
    ]

    core = r % 2
    wide = loc_cols // 2
    near = [(s, s ^ 1) for s in range(nrow)]
    halves, others = [], []
    for k in range(PIV):
        owner = order[k] // rb
        start = row_slot[k] * BS
        give = lax.dynamic_slice(matrix, (start, (1 - core) * wide), (BS, wide))
        keep = lax.dynamic_slice(matrix, (start, core * wide), (BS, wide))
        got = lax.ppermute(give, "row", near)
        part = jnp.where(owner % 2 == core, keep, got)
        hop = 2
        while hop < nrow:
            got = lax.ppermute(part, "row", [(s, s ^ hop) for s in range(nrow)])
            part = jnp.where((owner // hop) % 2 == (r // hop) % 2, part, got)
            hop *= 2
        halves.append(part)
        others.append(lax.ppermute(part, "row", near))

    def corner(x, y):
        orr, occ = order[x], order[y]
        block = lax.dynamic_slice(matrix, (row_slot[x] * BS, col_slot[y] * BS), (BS, BS))
        return jnp.where((orr // rb == r) & (occ // cb == c), block, 0.0)

    def square(make, xs, ys):
        return jnp.concatenate([jnp.concatenate([make(x, y) for y in ys], axis=1) for x in xs], axis=0)

    pair = [square(corner, (0, 1), (2, 3)), square(corner, (2, 3), (0, 1))]
    total = jnp.where(core == 0, pair[0], pair[1]) + lax.ppermute(
        jnp.where(core == 0, pair[1], pair[0]), "row", near
    )
    hop = 2
    while hop < nrow:
        total = total + lax.ppermute(total, "row", [(s, s ^ hop) for s in range(nrow)])
        hop *= 2
    total = total + sum(
        lax.ppermute(total, "col", [(s, (s + n) % ncol) for s in range(ncol)]) for n in range(1, ncol)
    )

    tables = lax.all_gather(jnp.concatenate([parent_of[:, None], child_map], axis=1), "front", axis=0, tiled=True)
    parents, maps = tables[:, 0], tables[:, 1:]
    pieces = lax.all_gather(children, "front", axis=0, tiled=True)
    early = PIV - 1
    pieces, total, halves[:early], *firsts = lax.optimization_barrier(
        (pieces, total, halves[:early], *[group[:early] for group in cands[1:]])
    )
    for group, first in zip(cands[1:], firsts):
        group[:early] = first
    owned = jnp.argmax((parents == lax.axis_index("front")).astype(i32)).astype(i32)
    own_map = lax.dynamic_index_in_dim(maps, owned, 0, keepdims=False)
    piece = lax.dynamic_index_in_dim(pieces, owned, 0, keepdims=True)
    kid = lax.all_gather(piece, ("row", "col"), axis=0, tiled=True)
    kid = kid.reshape(nrow, ncol, kr * BS, kc * BS)

    ids = jnp.arange(nb, dtype=i32)
    has = jnp.any(own_map[:, None] == ids[None, :], axis=0).astype(i32)
    src = jnp.maximum(jnp.sum((own_map[:, None] <= ids[None, :]).astype(i32), axis=0) - 1, 0)
    position = jnp.sum(jnp.where(order[:, None] == ids[None, :], ids[:, None], 0), axis=0).astype(i32)

    def rows_of(x):
        return lax.dynamic_slice_in_dim(x, r * rb, rb)

    def cols_of(x):
        return lax.dynamic_slice_in_dim(x, c * cb, cb)

    def picked(x):
        hit = (order[:PIV, None] == ids[None, :]).astype(i32)
        return jnp.sum(hit * x[None, :], axis=1)

    hit = (order[:PIV, None] == ids[None, :]).astype(i32)
    mask_cols = jnp.sum(hit[:, :, None] * mask.T[None], axis=1)
    mask_rows = jnp.sum(hit[:, :, None] * mask[None], axis=1)
    pos_r, pos_c = rows_of(position)[:, None], cols_of(position)[None, :]
    local_mask = lax.dynamic_slice(mask, (r * rb, c * cb), (rb, cb))
    kinds = jnp.where((pos_r >= 2) & (pos_c >= 2), 2, 1)
    kinds = jnp.where((pos_r >= 4) & (pos_c >= 4), 3, kinds)
    kinds = jnp.where(local_mask > 0, kinds, 0)
    kinds = jnp.where((pos_c < PIV) & (pos_r >= pos_c // 2 * 2 + 2), 4 + pos_c, kinds).astype(i32)

    partner = lax.ppermute(total, "row", near)
    corners = (jnp.where(core == 0, total, partner), jnp.where(core == 0, partner, total))
    psrc, phas = picked(src), picked(has)

    def kid_corner(x, y):
        a, b = psrc[x], psrc[y]
        block = lax.dynamic_slice(kid, (a // kr, b // kc, a % kr * BS, b % kc * BS), (1, 1, BS, BS))
        return jnp.where(phas[x] * phas[y] == 1, block[0, 0], 0.0)

    def mask_corner(x, y):
        return jnp.broadcast_to(picked(mask_rows[x])[y], (BS, BS)).astype(f32)

    u01 = (corners[0] + square(kid_corner, (0, 1), (2, 3))) * square(mask_corner, (0, 1), (2, 3))
    a10 = (corners[1] + square(kid_corner, (2, 3), (0, 1))) * square(mask_corner, (2, 3), (0, 1))
    l10 = jnp.dot(a10, diag_inverse[0, 0], precision=HIGH, preferred_element_type=f32)

    def pad(rows, n):
        return jnp.pad(rows.astype(i32), (0, n - rows.shape[0]))

    n = max(rb, PIV)
    zero = jnp.zeros((n,), i32)
    shift = jnp.stack([(c - order[k] // cb) % ncol for k in range(PIV)])
    meta = jnp.stack(
        [pad(shift, n), pad(psrc, n), pad(phas, n), pad(rows_of(src), n), pad(rows_of(has), n)]
        + [zero] * 3
        + [pad(rows_of(mask_cols[k]), n) for k in range(PIV)]
    )
    params = pltpu.CompilerParams(vmem_limit_bytes=52 * 2**20)

    def kid_spec(k):
        def where(i, m):
            a, b = m[3, i], m[1, k]
            return a // kr, b // kc, a % kr, b % kc

        return pl.BlockSpec((1, 1, BS, BS), where)

    low_h, low_l = pl.pallas_call(
        functools.partial(lower_kernel, others=ncol - 1, cols=cb),
        grid_spec=pltpu.PrefetchScalarGridSpec(
            num_scalar_prefetch=1,
            grid=(rb,),
            in_specs=[pl.BlockSpec((BS, BS), lambda i, m: (i, 0))] * (PIV * ncol)
            + [kid_spec(k) for k in range(PIV)]
            + [
                pl.BlockSpec((1, 2, 2 * BS, 2 * BS), lambda i, m: (0, 0, 0, 0)),
                pl.BlockSpec((2 * BS, 2 * BS), lambda i, m: (0, 0)),
            ],
            out_specs=[pl.BlockSpec((BS, PIV * BS), lambda i, m: (i, 0))] * 2,
        ),
        out_shape=[jax.ShapeDtypeStruct((loc_rows, PIV * BS), jnp.bfloat16)] * 2,
        compiler_params=params,
        name="lower",
    )(meta, *[x for group in cands for x in group], *[kid] * PIV, diag_inverse, u01)

    n = max(cb, PIV)
    zero = jnp.zeros((n,), i32)
    held = (jnp.arange(cb, dtype=i32) // (cb // 2) == core).astype(i32)
    meta = jnp.stack(
        [pad(held, n), pad(cols_of(src), n), pad(cols_of(has), n), pad(psrc, n), pad(phas, n)]
        + [pad(jnp.clip(jnp.arange(cb, dtype=i32) - lead * (cb // 2), 0, cb // 2 - 1), n) for lead in (core, 1 - core)]
        + [zero]
        + [pad(cols_of(mask_rows[k]), n) for k in range(PIV)]
    )

    def kid_spec_up(k):
        def where(j, m):
            a, b = m[3, k], m[1, j]
            return a // kr, b // kc, a % kr, b % kc

        return pl.BlockSpec((1, 1, BS, BS), where)

    up_h, up_l = pl.pallas_call(
        upper_kernel,
        grid_spec=pltpu.PrefetchScalarGridSpec(
            num_scalar_prefetch=1,
            grid=(cb,),
            in_specs=[pl.BlockSpec((BS, BS), lambda j, m: (0, m[5, j]))] * PIV
            + [pl.BlockSpec((BS, BS), lambda j, m: (0, m[6, j]))] * PIV
            + [kid_spec_up(k) for k in range(PIV)]
            + [pl.BlockSpec((2 * BS, 2 * BS), lambda j, m: (0, 0))],
            out_specs=[pl.BlockSpec((PIV * BS, BS), lambda j, m: (0, j))] * 2,
        ),
        out_shape=[jax.ShapeDtypeStruct((PIV * BS, loc_cols), jnp.bfloat16)] * 2,
        compiler_params=params,
        name="upper",
    )(meta, *halves, *others, *[kid] * PIV, l10)

    tile = min(4, cb)
    rows = jnp.stack([rows_of(has), rows_of(src)])
    cols = jnp.stack([cols_of(has), cols_of(src)])
    out = pl.pallas_call(
        functools.partial(trail_kernel, tile=tile, kc=kc),
        grid_spec=pltpu.PrefetchScalarGridSpec(
            num_scalar_prefetch=3,
            grid=(rb, cb // tile),
            in_specs=[
                pl.BlockSpec((BS, tile * BS), lambda i, t, rows, *_: (i, t)),
                pl.BlockSpec(
                    (1, ncol, BS, kc * BS), lambda i, t, rows, *_: (rows[1, i] // kr, 0, rows[1, i] % kr, 0)
                ),
                pl.BlockSpec((BS, PIV * BS), lambda i, t, *_: (i, 0)),
                pl.BlockSpec((BS, PIV * BS), lambda i, t, *_: (i, 0)),
                pl.BlockSpec(memory_space=pltpu.VMEM),
                pl.BlockSpec(memory_space=pltpu.VMEM),
            ],
            out_specs=pl.BlockSpec((BS, tile * BS), lambda i, t, *_: (i, t)),
        ),
        out_shape=jax.ShapeDtypeStruct((loc_rows, loc_cols), f32),
        compiler_params=params,
        name="trail",
    )(rows, cols, kinds, matrix, kid, low_h, low_l, up_h, up_l)
    return out[None]


def solution(mesh):
    placed = (
        P("front", "row", "col"),
        P("front", "row", "col"),
        P("front"),
        P("front", None),
        P("front", None, None),
        P("front", None),
        P("front", None, None, None),
    )
    return jax.shard_map(
        body, mesh=mesh, in_specs=placed, out_specs=P("front", "row", "col"), check_vma=False
    )
```
